256 devices in a mesh: amp: 64 (over y, z, core), slab: 4 (over x).
Axes of the slice: x: 4, y: 4, z: 8, core: 2. Of those that a mesh axis runs over, the one named last changes fastest.
Arguments:
- amplitudes: bfloat16 [4, 2048, 1024], P(None, 'amp', 'slab'), may hold values from -6 to 6
- integrals: bfloat16 [262144, 1024], P('amp', 'slab'), may hold values from -0.1875 to 0.1875
- ab_sizes: int32 [4], replicated, may hold values from 4096 to 126976, as said below
Outputs:
- residual: bfloat16 [2048, 262144], P('slab', 'amp')
The draws below stay inside these ranges and needn't reach their ends.
Inputs may be any that keep to these rules, and one draw needn't show every extreme that they name: `ab_sizes`: each irrep's ab rows form one consecutive block, in irrep order; every block has a multiple of 256 rows and at least 4096 rows, and the blocks sum to 262144 rows.
All inputs are finite; a program needn't handle non-finite values.
Results may differ from the reference program's by a relative error of at most 0.013.
Values may be sent and summed in bfloat16 or wider, within the bound.
No kernel may reach another device: no remote copies, remote signals or barrier semaphores. Data moves between devices by JAX's collectives and lax.ppermute only.
A program may use at most 128 MiB of HBM per device.

```python
import jax
import jax.numpy as jnp
from jax import lax

H = 4
IJ = 2048
CD = 1024
AB_DEV = 4096
ROWBLK = 256
SLAB_CD = 256
AB = 262144
N_AMP = 64


def draw_ab_sizes(key, part):
    key = jax.random.fold_in(key, 11)
    key_weights, key_big, key_empty = jax.random.split(key, 3)
    unit_blocks = AB_DEV // ROWBLK
    spare_blocks = N_AMP * unit_blocks - H * unit_blocks
    big_share = spare_blocks - spare_blocks // 2
    rest_share = spare_blocks // 2
    big_irrep = jax.random.randint(key_big, (), 0, H)
    empty_irrep = (big_irrep + 1 + jax.random.randint(key_empty, (), 0, H - 1)) % H
    irrep_ids = jnp.arange(H)
    weights = jax.random.randint(key_weights, (H,), 1, 5)
    weights = jnp.where((irrep_ids == empty_irrep) | (irrep_ids == big_irrep), 0, weights)
    shares = rest_share * weights // jnp.sum(weights)
    remainder = rest_share - jnp.sum(shares)
    taker = jnp.where((empty_irrep + 1) % H == big_irrep, (empty_irrep + 2) % H, (empty_irrep + 1) % H)
    shares = shares + jnp.where(irrep_ids == taker, remainder, 0)
    shares = shares + jnp.where(irrep_ids == big_irrep, big_share, 0)
    return ((unit_blocks + shares) * ROWBLK).astype(jnp.int32)


def block_scale(rng, extent, cuts, least, largest):
    def one(dim, blocks):
        draws = jax.random.uniform(jax.random.fold_in(jax.random.fold_in(rng, 6), dim), (blocks,), jnp.float32, least / len(cuts), largest / len(cuts))
        return jnp.repeat(jnp.exp(draws), extent[dim] // blocks).reshape((-1,) + (1,) * (len(extent) - dim - 1))

    loudness = one(*cuts[0])
    for cut in cuts[1:]:
        loudness = loudness * one(*cut)
    return loudness


def normal_values(own_key, extent, spread, limit, cuts=(), held_as=jnp.bfloat16):
    values = spread * jax.random.normal(own_key, extent, jnp.float32)
    if cuts:
        values = values * block_scale(own_key, extent, cuts, -0.22, 0.18)
    return jnp.clip(values, -limit, limit).astype(held_as)


def setup_inputs(seed: int = 0) -> dict:
    splits = jax.random.split(jax.random.key(seed), 4)
    amplitudes = normal_values(splits[0], (H, IJ, CD), 1.0, 6.0, ((1, 64), (2, 4)))
    integrals = normal_values(splits[1], (AB, CD), CD ** -0.5, 0.1875, ((0, 64), (1, 4)))
    ab_sizes = draw_ab_sizes(jax.random.fold_in(splits[3], 71), 0)
    return {"amplitudes": amplitudes, "integrals": integrals, "ab_sizes": ab_sizes}


def reference(amplitudes, integrals, ab_sizes):
    block_ends = jnp.cumsum(ab_sizes).astype(jnp.int32)
    block_count = AB // ROWBLK
    slab_count = CD // SLAB_CD
    block_starts = jnp.arange(block_count, dtype=jnp.int32) * ROWBLK
    irrep_label = jnp.sum((block_starts[:, None] >= block_ends[None, :]).astype(jnp.int32), axis=1)

    def ladder_block(inputs_pair):
        block_index, label = inputs_pair
        row_slice = lax.dynamic_slice_in_dim(integrals, (block_index * ROWBLK).astype(jnp.int32), ROWBLK, 0)
        row_slice = row_slice.astype(jnp.float32).reshape(ROWBLK, slab_count, SLAB_CD)
        amp_rows = lax.dynamic_index_in_dim(amplitudes, label, 0, keepdims=False)
        amp_rows = amp_rows.astype(jnp.float32).reshape(IJ, slab_count, SLAB_CD)
        partial_value = jnp.einsum('iqc,rqc->qir', amp_rows, row_slice)
        partial_value = lax.optimization_barrier(partial_value.astype(jnp.bfloat16)).astype(jnp.float32)
        return jnp.sum(partial_value, axis=0).astype(jnp.bfloat16)

    blocks = lax.map(ladder_block, (jnp.arange(block_count, dtype=jnp.int32), irrep_label))
    return jnp.transpose(blocks, (1, 0, 2)).reshape(IJ, AB)
```

```python
import functools

import jax
import jax.numpy as jnp
from jax import lax
from jax.experimental import pallas as pl
from jax.experimental.pallas import tpu as pltpu
from jax.sharding import PartitionSpec as P

ROWBLK = 256
N_AMP = 64
N_SLAB = 4
FWD = [(i, (i + 1) % N_SLAB) for i in range(N_SLAB)]
BWD = [(i, (i - 1) % N_SLAB) for i in range(N_SLAB)]
SWAP = [
    ((y * 16 + r) * N_SLAB + s, (s * 16 + r) * N_SLAB + y)
    for y in range(N_SLAB)
    for r in range(16)
    for s in range(N_SLAB)
]
SHIFT = [(i, i - 1) for i in range(1, N_AMP)]


def irrep_at(row_index, ends):
    return sum((row_index >= e).astype(jnp.int32) for e in ends)


def ladder_kernel(
    half_blocks, first, meta, own, a1, b1, a2, b2, c, d, amp_here, amp_next, *rest
):
    out = rest[-1]
    step = pl.program_id(0)
    low = step < half_blocks
    block = jnp.where(low, first + step, 8 + first + step - half_blocks)
    slot = meta[block]

    def product(amp, left, right, far):
        total = None
        for k, piece in enumerate((own, left, right, far)):
            part = lax.dot_general(
                amp[meta[16 + k]],
                piece[...],
                (((1,), (1,)), ((), ())),
                preferred_element_type=jnp.float32,
            )
            total = part if total is None else total + part
        out[...] = total.astype(out.dtype)

    @pl.when(low & (slot == 0))
    def _():
        product(amp_here, a1, b2, c)

    @pl.when(low & (slot != 0))
    def _():
        product(amp_next, a1, b2, c)

    @pl.when(jnp.logical_not(low) & (slot == 0))
    def _():
        product(amp_here, a2, b1, d)

    @pl.when(jnp.logical_not(low) & (slot != 0))
    def _():
        product(amp_next, a2, b1, d)


def ladder(meta, own, a1, b1, a2, b2, c, d, amp_here, amp_next, out, first):
    rows, width = own.shape
    pairs = amp_here.shape[1]
    n = c.shape[0] // ROWBLK
    where = lambda i: jnp.where(i < n, first + i, 8 + first + i - n)
    lo = lambda i: jnp.minimum(i, n - 1)
    hi = lambda i: jnp.maximum(i - n, 0)
    block = (ROWBLK, width)
    whole = pl.BlockSpec(amp_here.shape, lambda i, m: (0, 0, 0))
    in_specs = [
        pl.BlockSpec(block, lambda i, m: (where(i), 0)),
        pl.BlockSpec(block, lambda i, m: (first + lo(i), 0)),
        pl.BlockSpec(block, lambda i, m: (first + hi(i), 0)),
        pl.BlockSpec(block, lambda i, m: (first + hi(i), 0)),
        pl.BlockSpec(block, lambda i, m: (first + lo(i), 0)),
        pl.BlockSpec(block, lambda i, m: (lo(i), 0)),
        pl.BlockSpec(block, lambda i, m: (hi(i), 0)),
        whole,
        whole,
    ]
    args = [meta, own, a1, b1, a2, b2, c, d, amp_here, amp_next]
    aliases = {}
    if out is not None:
        in_specs.append(pl.BlockSpec(memory_space=pl.ANY))
        aliases = {len(args): 0}
        args.append(out)
    return pl.pallas_call(
        functools.partial(ladder_kernel, n, first),
        grid_spec=pltpu.PrefetchScalarGridSpec(
            num_scalar_prefetch=1,
            grid=(2 * n,),
            in_specs=in_specs,
            out_specs=pl.BlockSpec((pairs, ROWBLK), lambda i, m: (0, where(i))),
        ),
        out_shape=jax.ShapeDtypeStruct((pairs, rows), jnp.bfloat16),
        input_output_aliases=aliases,
        cost_estimate=pl.CostEstimate(
            flops=2 * pairs * 2 * n * ROWBLK * 4 * width,
            bytes_accessed=2 * n * ROWBLK * (4 * width + pairs) * 2,
            transcendentals=0,
        ),
        compiler_params=pltpu.CompilerParams(vmem_limit_bytes=24 * 1024 * 1024),
        name=f"ladder_{first}",
    )(*args)


def body(amplitudes, integrals, ab_sizes):
    rows, width = integrals.shape
    me = lax.axis_index("amp")
    slab = lax.axis_index("slab")
    e0 = ab_sizes[0]
    e1 = e0 + ab_sizes[1]
    ends = (e0, e1, e1 + ab_sizes[2])

    half = rows // 2
    low, high = integrals[:half], integrals[half:]
    a1 = lax.ppermute(low, "slab", FWD)
    b1 = lax.ppermute(high, "slab", BWD)

    held = lax.ppermute(amplitudes, ("amp", "slab"), SWAP)
    owner_first = irrep_at(jnp.arange(N_AMP, dtype=jnp.int32) * rows, ends)
    pick = owner_first[:, None, None]
    outgoing = jnp.where(
        pick == 0,
        held[0][None],
        jnp.where(pick == 1, held[1][None], jnp.where(pick == 2, held[2][None], held[3][None])),
    )
    high2, low2, outgoing = lax.optimization_barrier((high, low, outgoing))
    a2 = lax.ppermute(high2, "slab", FWD)
    b2 = lax.ppermute(low2, "slab", BWD)
    got = lax.all_to_all(outgoing, "amp", split_axis=0, concat_axis=0, tiled=True)
    amp_here = got.reshape(N_SLAB, -1, width)
    amp_next = lax.ppermute(got, "amp", SHIFT).reshape(N_SLAB, -1, width)

    quarter = half // 2
    c1 = lax.ppermute(a1[:quarter], "slab", FWD)
    d1 = lax.ppermute(b1[:quarter], "slab", BWD)
    c2 = lax.ppermute(a1[quarter:], "slab", FWD)
    d2 = lax.ppermute(b1[quarter:], "slab", BWD)

    start = me * rows
    mine = irrep_at(start, ends)
    blocks = start + jnp.arange(rows // ROWBLK, dtype=jnp.int32) * ROWBLK
    slot = (irrep_at(blocks, ends) != mine).astype(jnp.int32)
    places = (slab + jnp.array([0, N_SLAB - 1, 1, 2], jnp.int32)) % N_SLAB
    meta = jnp.concatenate([slot, places])

    out = ladder(meta, integrals, a1, b1, a2, b2, c1, d1, amp_here, amp_next, None, 0)
    return ladder(meta, integrals, a1, b1, a2, b2, c2, d2, amp_here, amp_next, out, 4)


def solution(mesh):
    placed = (P(None, "amp", "slab"), P("amp", "slab"), P())
    return jax.shard_map(
        body, mesh=mesh, in_specs=placed, out_specs=P("slab", "amp"), check_vma=False
    )
```

```python
import functools

import jax
import jax.numpy as jnp
from jax import lax
from jax.experimental import pallas as pl
from jax.experimental.pallas import tpu as pltpu
from jax.sharding import PartitionSpec as P

ROWBLK = 256
N_AMP = 64
HALVES = 2
N_SLAB = 4
N_Y = 4
PER_Y = 16
FWD = [(i, (i + 1) % N_SLAB) for i in range(N_SLAB)]
BWD = [(i, (i - 1) % N_SLAB) for i in range(N_SLAB)]
SWAP = [
    ((y * PER_Y + r) * N_SLAB + s, (s * PER_Y + r) * N_SLAB + y)
    for y in range(N_Y)
    for r in range(PER_Y)
    for s in range(N_SLAB)
]
Y_SHIFT = [
    [(y * PER_Y + r, ((y + k) % N_Y) * PER_Y + r) for y in range(N_Y) for r in range(PER_Y)]
    for k in range(N_Y)
]
Y_GROUPS = [[y * PER_Y + r for r in range(PER_Y)] for y in range(N_Y)]
BEFORE = [(i, i - 1) for i in range(1, N_AMP)]


def after(value, *others):
    return lax.optimization_barrier((value,) + others)[0]


def irrep_at(row, sizes):
    first = sizes[0]
    second = first + sizes[1]
    third = second + sizes[2]
    one = lambda end: (row >= end).astype(jnp.int32)
    return one(first) + one(second) + one(third)


def pick_kernel(rows, sizes, place, *refs):
    columns, out = refs[:-1], refs[-1]
    y = place[0] // PER_Y
    for d in range(PER_Y):
        h = irrep_at((y * PER_Y + d) * rows, sizes)
        for k, column in enumerate(columns):
            out[d, lax.rem(y + 2 * N_SLAB - place[1] - k, N_SLAB)] = column[h]


def pick(sizes, place, columns, rows):
    vmem = pl.BlockSpec(memory_space=pltpu.VMEM)
    smem = pl.BlockSpec(memory_space=pltpu.SMEM)
    _, pairs, width = columns[0].shape
    shape = (PER_Y, len(columns), pairs, width)
    return pl.pallas_call(
        functools.partial(pick_kernel, rows),
        in_specs=[smem, smem] + [vmem] * len(columns),
        out_specs=vmem,
        out_shape=jax.ShapeDtypeStruct(shape, columns[0].dtype),
        cost_estimate=pl.CostEstimate(flops=0, bytes_accessed=3 << 20, transcendentals=0),
        name="pick",
    )(sizes, place, *columns)


def ladder_kernel(rows, runs, sizes, place, own, below, above, *refs):
    fars, amps, out = refs[: len(runs)], refs[len(runs) : len(runs) + 2 * HALVES], refs[-1]
    step = pl.program_id(0)
    step_rows = own.shape[0]
    start = place[0] * rows
    mine = irrep_at(start, sizes)
    row, far, done = runs[0][0] + step * step_rows, fars[0][...], runs[0][1]
    for (begin, steps), piece in zip(runs[1:], fars[1:]):
        row = jnp.where(step < done, row, begin + (step - done) * step_rows)
        far = jnp.where(step < done, far, piece[...])
        done += steps

    def product(parts, at):
        pairs = parts[0].shape[0] * parts[0].shape[2]
        for m, amp in enumerate(parts):
            total = None
            for k, piece in enumerate((own[at, :], below[at, :], far[at], above[at, :])):
                part = lax.dot_general(
                    amp[:, k].reshape(pairs, amp.shape[-1]),
                    piece,
                    (((1,), (1,)), ((), ())),
                    preferred_element_type=jnp.float32,
                )
                total = part if total is None else total + part
            out[m * pairs : (m + 1) * pairs, at] = total.astype(out.dtype)

    same = irrep_at(start + row + step_rows - 1, sizes) == mine

    @pl.when(same)
    def _():
        product(amps[:HALVES], slice(0, step_rows))

    @pl.when(jnp.logical_not(same))
    def _():
        for h in range(step_rows // ROWBLK):
            at = slice(h * ROWBLK, (h + 1) * ROWBLK)
            here = irrep_at(start + row + h * ROWBLK, sizes) == mine

            @pl.when(here)
            def _(at=at):
                product(amps[:HALVES], at)

            @pl.when(jnp.logical_not(here))
            def _(at=at):
                product(amps[HALVES:], at)


def ladder(sizes, place, own, below, above, fars, amps, out, step_rows):
    rows, width = own.shape
    pairs = HALVES * amps[0].shape[0] * amps[0].shape[2]
    runs = [(row, far.shape[0] // step_rows) for far, row in fars]
    bases = [sum(n for _, n in runs[:k]) for k in range(len(runs))]

    def where(i):
        at = i + runs[0][0] // step_rows
        for (row, _), base in zip(runs[1:], bases[1:]):
            at = jnp.where(i < base, at, i - base + row // step_rows)
        return at

    block = (step_rows, width)
    in_specs = [pl.BlockSpec(block, lambda i, *_: (where(i), 0))] * 3
    for (_, n), base in zip(runs, bases):
        in_specs.append(
            pl.BlockSpec(block, lambda i, *_, n=n, base=base: (jnp.clip(i - base, 0, n - 1), 0))
        )
    in_specs += [pl.BlockSpec(a.shape, lambda i, *_: (0, 0, 0, 0)) for a in amps]
    args = [sizes, place, own, below, above, *(far for far, _ in fars), *amps]
    aliases = {}
    if out is not None:
        in_specs.append(pl.BlockSpec(memory_space=pl.ANY))
        aliases = {len(args): 0}
        args.append(out)
    steps = sum(n for _, n in runs)
    return pl.pallas_call(
        functools.partial(ladder_kernel, rows, runs),
        grid_spec=pltpu.PrefetchScalarGridSpec(
            num_scalar_prefetch=2,
            grid=(steps,),
            in_specs=in_specs,
            out_specs=pl.BlockSpec((pairs, step_rows), lambda i, *_: (0, where(i))),
        ),
        out_shape=jax.ShapeDtypeStruct((pairs, rows), jnp.bfloat16),
        input_output_aliases=aliases,
        cost_estimate=pl.CostEstimate(
            flops=2 * pairs * steps * step_rows * 4 * width,
            bytes_accessed=steps * step_rows * (4 * width + pairs) * 2,
            transcendentals=0,
        ),
        compiler_params=pltpu.CompilerParams(vmem_limit_bytes=16 * 1024 * 1024),
        name="ladder",
    )(*args)


def body(amplitudes, integrals, sizes):
    rows, width = integrals.shape
    place = jnp.stack([lax.axis_index("amp"), lax.axis_index("slab")]).astype(jnp.int32)
    up = lambda v: lax.ppermute(v, "slab", FWD)
    down = lambda v: lax.ppermute(v, "slab", BWD)
    half = rows // 2

    held = lax.ppermute(amplitudes, ("amp", "slab"), SWAP)
    columns = [held] + [lax.ppermute(held, "amp", Y_SHIFT[k]) for k in (1, 2, 3)]

    above, below = up(integrals), down(integrals)
    groups = [[(0, 3 * rows // 8)], [(3 * rows // 8, half)]]
    far = {}
    for s, e in (span for group in groups for span in group):
        far[s] = (up(above[s:e]), s)
        far[rows - e] = (down(below[rows - e : rows - s]), rows - e)

    outgoing = pick(sizes, place, columns, rows)
    arrived = lax.all_to_all(
        outgoing, "amp", split_axis=0, concat_axis=0, axis_index_groups=Y_GROUPS, tiled=True
    )
    n = PER_Y // HALVES
    amps_here = [arrived[m * n : (m + 1) * n] for m in range(HALVES)]
    amps_next = [lax.ppermute(after(v, above, below), "amp", BEFORE) for v in amps_here]
    amps = amps_here + amps_next

    out = None
    for group in groups:
        fars = [far[s] for s, _ in group] + [far[rows - e] for _, e in group]
        out = ladder(sizes, place, integrals, below, above, fars, amps, out, 512)
    return out


def solution(mesh):
    placed = (P(None, "amp", "slab"), P("amp", "slab"), P())
    return jax.shard_map(
        body, mesh=mesh, in_specs=placed, out_specs=P("slab", "amp"), check_vma=False
    )
```

```python
import functools

import jax
import jax.numpy as jnp
from jax import lax
from jax.experimental import pallas as pl
from jax.experimental.pallas import tpu as pltpu
from jax.sharding import PartitionSpec as P

ROWBLK = 256
N_AMP = 64
HALVES = 2
N_SLAB = 4
N_Y = 4
PER_Y = 16
FWD = [(i, (i + 1) % N_SLAB) for i in range(N_SLAB)]
BWD = [(i, (i - 1) % N_SLAB) for i in range(N_SLAB)]
SWAP = [
    ((y * PER_Y + r) * N_SLAB + s, (s * PER_Y + r) * N_SLAB + y)
    for y in range(N_Y)
    for r in range(PER_Y)
    for s in range(N_SLAB)
]
Y_SHIFT = [
    [(y * PER_Y + r, ((y + k) % N_Y) * PER_Y + r) for y in range(N_Y) for r in range(PER_Y)]
    for k in range(N_Y)
]
Y_GROUPS = [[y * PER_Y + r for r in range(PER_Y)] for y in range(N_Y)]
BEFORE = [(i, i - 1) for i in range(1, N_AMP)]


def after(value, *others):
    return lax.optimization_barrier((value,) + others)[0]


def irrep_at(row, sizes):
    first = sizes[0]
    second = first + sizes[1]
    third = second + sizes[2]
    one = lambda end: (row >= end).astype(jnp.int32)
    return one(first) + one(second) + one(third)


def pick_kernel(rows, sizes, place, *refs):
    columns, out = refs[:-1], refs[-1]
    y = place[0] // PER_Y
    for d in range(PER_Y):
        h = irrep_at((y * PER_Y + d) * rows, sizes)
        for k, column in enumerate(columns):
            out[d, lax.rem(y + 2 * N_SLAB - place[1] - k, N_SLAB)] = column[h]


def pick(sizes, place, columns, rows):
    vmem = pl.BlockSpec(memory_space=pltpu.VMEM)
    smem = pl.BlockSpec(memory_space=pltpu.SMEM)
    _, pairs, width = columns[0].shape
    shape = (PER_Y, len(columns), pairs, width)
    return pl.pallas_call(
        functools.partial(pick_kernel, rows),
        in_specs=[smem, smem] + [vmem] * len(columns),
        out_specs=vmem,
        out_shape=jax.ShapeDtypeStruct(shape, columns[0].dtype),
        cost_estimate=pl.CostEstimate(flops=0, bytes_accessed=3 << 20, transcendentals=0),
        name="pick",
    )(sizes, place, *columns)


def ladder_kernel(rows, runs, sizes, place, own, below, above, *refs):
    fars, amps, out = refs[: len(runs)], refs[len(runs) : len(runs) + 2 * HALVES], refs[-1]
    step = pl.program_id(0)
    step_rows = own.shape[0]
    start = place[0] * rows
    mine = irrep_at(start, sizes)
    row, far, done = runs[0][0] + step * step_rows, fars[0][...], runs[0][1]
    for (begin, steps), piece in zip(runs[1:], fars[1:]):
        row = jnp.where(step < done, row, begin + (step - done) * step_rows)
        far = jnp.where(step < done, far, piece[...])
        done += steps

    def product(parts, at):
        pairs = parts[0].shape[0] * parts[0].shape[2]
        for m, amp in enumerate(parts):
            total = None
            for k, piece in enumerate((own[at, :], below[at, :], far[at], above[at, :])):
                part = lax.dot_general(
                    amp[:, k].reshape(pairs, amp.shape[-1]),
                    piece,
                    (((1,), (1,)), ((), ())),
                    preferred_element_type=jnp.float32,
                )
                total = part if total is None else total + part
            out[m * pairs : (m + 1) * pairs, at] = total.astype(out.dtype)

    same = irrep_at(start + row + step_rows - 1, sizes) == mine

    @pl.when(same)
    def _():
        product(amps[:HALVES], slice(0, step_rows))

    @pl.when(jnp.logical_not(same))
    def _():
        for h in range(step_rows // ROWBLK):
            at = slice(h * ROWBLK, (h + 1) * ROWBLK)
            here = irrep_at(start + row + h * ROWBLK, sizes) == mine

            @pl.when(here)
            def _(at=at):
                product(amps[:HALVES], at)

            @pl.when(jnp.logical_not(here))
            def _(at=at):
                product(amps[HALVES:], at)


def ladder(sizes, place, own, below, above, fars, amps, out, step_rows):
    rows, width = own.shape
    pairs = HALVES * amps[0].shape[0] * amps[0].shape[2]
    runs = [(row, far.shape[0] // step_rows) for far, row in fars]
    bases = [sum(n for _, n in runs[:k]) for k in range(len(runs))]

    def where(i):
        at = runs[0][0] + i * step_rows
        for (row, _), base in zip(runs[1:], bases[1:]):
            at = jnp.where(i < base, at, row + (i - base) * step_rows)
        return pl.multiple_of(at, ROWBLK)

    block = (step_rows, width)
    rows_at = (pl.Element(step_rows), pl.Element(width))
    in_specs = [pl.BlockSpec(rows_at, lambda i, *_: (where(i), 0))] * 3
    for (_, n), base in zip(runs, bases):
        in_specs.append(
            pl.BlockSpec(block, lambda i, *_, n=n, base=base: (jnp.clip(i - base, 0, n - 1), 0))
        )
    in_specs += [pl.BlockSpec(a.shape, lambda i, *_: (0, 0, 0, 0)) for a in amps]
    args = [sizes, place, own, below, above, *(far for far, _ in fars), *amps]
    aliases = {}
    if out is not None:
        in_specs.append(pl.BlockSpec(memory_space=pl.ANY))
        aliases = {len(args): 0}
        args.append(out)
    steps = sum(n for _, n in runs)
    return pl.pallas_call(
        functools.partial(ladder_kernel, rows, runs),
        grid_spec=pltpu.PrefetchScalarGridSpec(
            num_scalar_prefetch=2,
            grid=(steps,),
            in_specs=in_specs,
            out_specs=pl.BlockSpec(
                (pl.Element(pairs), pl.Element(step_rows)), lambda i, *_: (0, where(i))
            ),
        ),
        out_shape=jax.ShapeDtypeStruct((pairs, rows), jnp.bfloat16),
        input_output_aliases=aliases,
        cost_estimate=pl.CostEstimate(
            flops=2 * pairs * steps * step_rows * 4 * width,
            bytes_accessed=steps * step_rows * (4 * width + pairs) * 2,
            transcendentals=0,
        ),
        compiler_params=pltpu.CompilerParams(vmem_limit_bytes=24 * 1024 * 1024),
        name="ladder",
    )(*args)


def body(amplitudes, integrals, sizes):
    rows, width = integrals.shape
    place = jnp.stack([lax.axis_index("amp"), lax.axis_index("slab")]).astype(jnp.int32)
    up = lambda v: lax.ppermute(v, "slab", FWD)
    down = lambda v: lax.ppermute(v, "slab", BWD)
    half = rows // 2

    held = lax.ppermute(amplitudes, ("amp", "slab"), SWAP)
    columns = [held] + [lax.ppermute(held, "amp", Y_SHIFT[k]) for k in (1, 2, 3)]

    above, below = up(integrals), down(integrals)
    groups = [[(0, 3 * rows // 8)], [(3 * rows // 8, half)]]
    far = {}
    for s, e in (span for group in groups for span in group):
        far[s] = (up(above[s:e]), s)
        far[rows - e] = (down(below[rows - e : rows - s]), rows - e)

    outgoing = pick(sizes, place, columns, rows)
    arrived = lax.all_to_all(
        outgoing, "amp", split_axis=0, concat_axis=0, axis_index_groups=Y_GROUPS, tiled=True
    )
    n = PER_Y // HALVES
    amps_here = [arrived[m * n : (m + 1) * n] for m in range(HALVES)]
    amps_next = [lax.ppermute(after(v, above, below), "amp", BEFORE) for v in amps_here]
    amps = amps_here + amps_next

    out = None
    for group, step_rows in zip(groups, (768, 512)):
        fars = [far[s] for s, _ in group] + [far[rows - e] for _, e in group]
        out = ladder(sizes, place, integrals, below, above, fars, amps, out, step_rows)
    return out


def solution(mesh):
    placed = (P(None, "amp", "slab"), P("amp", "slab"), P())
    return jax.shard_map(
        body, mesh=mesh, in_specs=placed, out_specs=P("slab", "amp"), check_vma=False
    )
```

```python
import functools

import jax
import jax.numpy as jnp
from jax import lax
from jax.experimental import pallas as pl
from jax.experimental.pallas import tpu as pltpu
from jax.sharding import PartitionSpec as P

ROWBLK = 256
N_AMP = 64
HALVES = 2
N_SLAB = 4
N_Y = 4
PER_Y = 16
FWD = [(i, (i + 1) % N_SLAB) for i in range(N_SLAB)]
BWD = [(i, (i - 1) % N_SLAB) for i in range(N_SLAB)]
SWAP = [
    ((y * PER_Y + r) * N_SLAB + s, (s * PER_Y + r) * N_SLAB + y)
    for y in range(N_Y)
    for r in range(PER_Y)
    for s in range(N_SLAB)
]
Y_SHIFT = [
    [(y * PER_Y + r, ((y + k) % N_Y) * PER_Y + r) for y in range(N_Y) for r in range(PER_Y)]
    for k in range(N_Y)
]
Y_GROUPS = [[y * PER_Y + r for r in range(PER_Y)] for y in range(N_Y)]
BEFORE = [(i, i - 1) for i in range(1, N_AMP)]


def after(value, *others):
    return lax.optimization_barrier((value,) + others)[0]


def irrep_at(row, sizes):
    first = sizes[0]
    second = first + sizes[1]
    third = second + sizes[2]
    one = lambda end: (row >= end).astype(jnp.int32)
    return one(first) + one(second) + one(third)


def pick_kernel(rows, sizes, place, *refs):
    columns, out = refs[:-1], refs[-1]
    y = place[0] // PER_Y
    for d in range(PER_Y):
        h = irrep_at((y * PER_Y + d) * rows, sizes)
        for k, column in enumerate(columns):
            out[d, lax.rem(y + 2 * N_SLAB - place[1] - k, N_SLAB)] = column[h]


def pick(sizes, place, columns, rows):
    vmem = pl.BlockSpec(memory_space=pltpu.VMEM)
    smem = pl.BlockSpec(memory_space=pltpu.SMEM)
    _, pairs, width = columns[0].shape
    shape = (PER_Y, len(columns), pairs, width)
    return pl.pallas_call(
        functools.partial(pick_kernel, rows),
        in_specs=[smem, smem] + [vmem] * len(columns),
        out_specs=vmem,
        out_shape=jax.ShapeDtypeStruct(shape, columns[0].dtype),
        cost_estimate=pl.CostEstimate(flops=8000000000, bytes_accessed=3 << 20, transcendentals=0),
        name="pick",
    )(sizes, place, *columns)


def ladder_kernel(rows, runs, sizes, place, own, below, above, *refs):
    fars, amps, out = refs[: len(runs)], refs[len(runs) : len(runs) + 2 * HALVES], refs[-1]
    step = pl.program_id(0)
    step_rows = own.shape[0]
    start = place[0] * rows
    mine = irrep_at(start, sizes)
    row, far, done = runs[0][0] + step * step_rows, fars[0][...], runs[0][1]
    for (begin, steps), piece in zip(runs[1:], fars[1:]):
        row = jnp.where(step < done, row, begin + (step - done) * step_rows)
        far = jnp.where(step < done, far, piece[...])
        done += steps

    def product(parts, at):
        pairs = parts[0].shape[0] * parts[0].shape[2]
        for m, amp in enumerate(parts):
            total = None
            for k, piece in enumerate((own[at, :], below[at, :], far[at], above[at, :])):
                part = lax.dot_general(
                    amp[:, k].reshape(pairs, amp.shape[-1]),
                    piece,
                    (((1,), (1,)), ((), ())),
                    preferred_element_type=jnp.float32,
                )
                total = part if total is None else total + part
            out[m * pairs : (m + 1) * pairs, at] = total.astype(out.dtype)

    same = irrep_at(start + row + step_rows - 1, sizes) == mine

    @pl.when(same)
    def _():
        product(amps[:HALVES], slice(0, step_rows))

    @pl.when(jnp.logical_not(same))
    def _():
        for h in range(step_rows // ROWBLK):
            at = slice(h * ROWBLK, (h + 1) * ROWBLK)
            here = irrep_at(start + row + h * ROWBLK, sizes) == mine

            @pl.when(here)
            def _(at=at):
                product(amps[:HALVES], at)

            @pl.when(jnp.logical_not(here))
            def _(at=at):
                product(amps[HALVES:], at)


def ladder(sizes, place, own, below, above, fars, amps, out, step_rows):
    rows, width = own.shape
    pairs = HALVES * amps[0].shape[0] * amps[0].shape[2]
    runs = [(row, far.shape[0] // step_rows) for far, row in fars]
    bases = [sum(n for _, n in runs[:k]) for k in range(len(runs))]

    def where(i):
        at = runs[0][0] + i * step_rows
        for (row, _), base in zip(runs[1:], bases[1:]):
            at = jnp.where(i < base, at, row + (i - base) * step_rows)
        return pl.multiple_of(at, ROWBLK)

    block = (step_rows, width)
    rows_at = (pl.Element(step_rows), pl.Element(width))
    in_specs = [pl.BlockSpec(rows_at, lambda i, *_: (where(i), 0))] * 3
    for (_, n), base in zip(runs, bases):
        in_specs.append(
            pl.BlockSpec(block, lambda i, *_, n=n, base=base: (jnp.clip(i - base, 0, n - 1), 0))
        )
    in_specs += [pl.BlockSpec(a.shape, lambda i, *_: (0, 0, 0, 0)) for a in amps]
    args = [sizes, place, own, below, above, *(far for far, _ in fars), *amps]
    aliases = {}
    if out is not None:
        in_specs.append(pl.BlockSpec(memory_space=pl.ANY))
        aliases = {len(args): 0}
        args.append(out)
    steps = sum(n for _, n in runs)
    return pl.pallas_call(
        functools.partial(ladder_kernel, rows, runs),
        grid_spec=pltpu.PrefetchScalarGridSpec(
            num_scalar_prefetch=2,
            grid=(steps,),
            in_specs=in_specs,
            out_specs=pl.BlockSpec(
                (pl.Element(pairs), pl.Element(step_rows)), lambda i, *_: (0, where(i))
            ),
        ),
        out_shape=jax.ShapeDtypeStruct((pairs, rows), jnp.bfloat16),
        input_output_aliases=aliases,
        cost_estimate=pl.CostEstimate(
            flops=2 * pairs * steps * step_rows * 4 * width,
            bytes_accessed=steps * step_rows * (4 * width + pairs) * 2,
            transcendentals=0,
        ),
        compiler_params=pltpu.CompilerParams(vmem_limit_bytes=24 * 1024 * 1024),
        name="ladder",
    )(*args)


def body(amplitudes, integrals, sizes):
    rows, width = integrals.shape
    place = jnp.stack([lax.axis_index("amp"), lax.axis_index("slab")]).astype(jnp.int32)
    up = lambda v: lax.ppermute(v, "slab", FWD)
    down = lambda v: lax.ppermute(v, "slab", BWD)
    half = rows // 2

    held = lax.ppermute(amplitudes, ("amp", "slab"), SWAP)
    columns = [held] + [lax.ppermute(held, "amp", Y_SHIFT[k]) for k in (1, 2, 3)]

    above, below = up(integrals), down(integrals)
    groups = [[(0, rows // 4)], [(rows // 4, half)]]
    far = {}
    for s, e in (span for group in groups for span in group):
        far[s] = (up(above[s:e]), s)
        far[rows - e] = (down(below[rows - e : rows - s]), rows - e)

    outgoing = pick(sizes, place, columns, rows)
    arrived = lax.all_to_all(
        outgoing, "amp", split_axis=0, concat_axis=0, axis_index_groups=Y_GROUPS, tiled=True
    )
    n = PER_Y // HALVES
    amps_here = [arrived[m * n : (m + 1) * n] for m in range(HALVES)]
    amps_next = [lax.ppermute(after(v, above, below), "amp", BEFORE) for v in amps_here]
    amps = amps_here + amps_next

    out = None
    for group, step_rows in zip(groups, (1024, 1024)):
        fars = [far[s] for s, _ in group] + [far[rows - e] for _, e in group]
        out = ladder(sizes, place, integrals, below, above, fars, amps, out, step_rows)
    return out


def solution(mesh):
    placed = (P(None, "amp", "slab"), P("amp", "slab"), P())
    return jax.shard_map(
        body, mesh=mesh, in_specs=placed, out_specs=P("slab", "amp"), check_vma=False
    )
```
